512 devices in a mesh: row: 32 (over y_lo, z, core), col: 16 (over y_hi, x).
Axes of the slice: x: 4, y: 8 (y_hi: 4, y_lo: 2; y = y_hi * 2 + y_lo), z: 8, core: 2. Of those that a mesh axis runs over, the one named last changes fastest.
Arguments:
- a_tiles: bfloat16 [32, 16, 2, 16, 128, 128], P('row', 'col'), may hold values from 0 to 0.25
- a_index: int32 [32, 16, 2, 16], P('row', 'col'), may hold values from 0 to 127, as said below
- a_count: int32 [32, 16, 2], P('row', 'col'), may hold values from 1 to 16
- b_tiles: bfloat16 [32, 16, 16, 128, 128], P('row', 'col'), may hold values from 0 to 0.25
- b_index: int32 [32, 16, 16], P('row', 'col'), may hold values from 0 to 127, as said below
- b_count: int32 [32, 16], P('row', 'col'), may hold values from 1 to 16
- c_partial: float32 [16384, 8192], P('row', 'col'), may hold values from 0.25 to 60, as said below
- prune_mask: int32 [128, 64], P('row', 'col'), may hold values from 0 to 1, as said below
Outputs:
- renormed: float32 [16384, 8192], P('row', 'col')
The draws below stay inside these ranges and needn't reach their ends.
Inputs may be any that keep to these rules, and one draw needn't show every extreme that they name: `a_index`: within one device and section the slots are distinct. `b_index`: within one device the slots are distinct. `prune_mask`: every block column keeps at least one tile. `c_partial`: positive entries.
All inputs are finite; a program needn't handle non-finite values.
Results may differ from the reference program's by a relative error of at most 0.0003.
Values may be sent and summed in bfloat16 or wider, within the bound.
No kernel may reach another device: no remote copies, remote signals or barrier semaphores. Data moves between devices by JAX's collectives and lax.ppermute only.
A program may use at most 64 MiB of HBM per device.

```python
import jax
import jax.numpy as jnp
from jax import lax

TILE = 128
MB = 4
NB = 4
W = 32
KA = 16
KB = 16
SECTIONS = 2
ROWS = 16384
COLS = 8192
RB = 128
CB = 64
N_ROW = 32
N_COL = 16


def draw_a_index(key, part):
    key = jax.random.fold_in(key, 11)
    keys = jax.random.split(key, N_ROW * N_COL * SECTIONS)
    picks = jax.vmap(lambda k: jax.random.permutation(k, MB * W)[:KA])(keys)
    return picks.reshape(N_ROW, N_COL, SECTIONS, KA).astype(jnp.int32)


def draw_a_count(key, part):
    key = jax.random.fold_in(key, 12)
    counts = jax.random.randint(key, (N_ROW, N_COL, SECTIONS), 1, KA + 1)
    counts = counts.at[0, N_COL - 1, 0].set(KA)
    counts = counts.at[N_ROW - 1, N_COL - 1, 1].set(1)
    return counts.astype(jnp.int32)


def draw_b_index(key, part):
    key = jax.random.fold_in(key, 13)
    keys = jax.random.split(key, N_ROW * N_COL)
    picks = jax.vmap(lambda k: jax.random.permutation(k, W * NB)[:KB])(keys)
    return picks.reshape(N_ROW, N_COL, KB).astype(jnp.int32)


def draw_b_count(key, part):
    key = jax.random.fold_in(key, 14)
    counts = jax.random.randint(key, (N_ROW, N_COL), 1, KB + 1)
    counts = counts.at[N_ROW - 2, 0].set(KB)
    counts = counts.at[N_ROW - 1, N_COL - 1].set(1)
    return counts.astype(jnp.int32)


def draw_prune_mask(key, part):
    key = jax.random.fold_in(key, 15)
    coins = jax.random.randint(key, (RB, CB), 0, 2)
    forced = (jnp.arange(RB)[:, None] == jnp.arange(CB)[None, :]).astype(jnp.int32)
    return jnp.maximum(coins, forced).astype(jnp.int32)


def draw_c_partial(key, part):
    key = jax.random.fold_in(key, 16)
    first = jax.random.fold_in(key, 0)
    rising = 1.0 + 2.0 * jnp.arange(ROWS, dtype=jnp.float32) / (ROWS - 1)
    base = jax.random.uniform(first, (ROWS, COLS), jnp.float32, 0.5, 1.5)
    return (base * rising[:, None]).astype(jnp.float32)


def level_of(rng, dims, pieces, least, largest):
    level = 1.0
    for dim, blocks in pieces:
        heights = jax.random.uniform(jax.random.fold_in(jax.random.fold_in(rng, 6), dim), (blocks,), jnp.float32, least / len(pieces), largest / len(pieces))
        level = level * jnp.repeat(jnp.exp(heights), dims[dim] // blocks).reshape((-1,) + (1,) * (len(dims) - 1 - dim))
    return level


def setup_inputs(seed: int = 0) -> dict:
    arg_keys = jax.random.split(jax.random.key(seed), 9)
    return {
        "a_tiles": jnp.clip(0.25 * jax.random.uniform(arg_keys[0], (N_ROW, N_COL, SECTIONS, KA, TILE, TILE), jnp.float32) ** level_of(arg_keys[0], (N_ROW, N_COL, SECTIONS, KA, TILE, TILE), ((0, 32), (1, 16)), -0.2, 0.2), 0.0, 0.25).astype(jnp.bfloat16),
        "a_index": draw_a_index(jax.random.fold_in(arg_keys[8], 71), 0),
        "a_count": draw_a_count(jax.random.fold_in(arg_keys[8], 71), 0),
        "b_tiles": jnp.clip(0.25 * jax.random.uniform(arg_keys[3], (N_ROW, N_COL, KB, TILE, TILE), jnp.float32) ** level_of(arg_keys[3], (N_ROW, N_COL, KB, TILE, TILE), ((0, 32), (1, 16)), -0.2, 0.2), 0.0, 0.25).astype(jnp.bfloat16),
        "b_index": draw_b_index(jax.random.fold_in(arg_keys[8], 71), 0),
        "b_count": draw_b_count(jax.random.fold_in(arg_keys[8], 71), 0),
        "c_partial": draw_c_partial(jax.random.fold_in(arg_keys[8], 71), 0),
        "prune_mask": draw_prune_mask(jax.random.fold_in(arg_keys[8], 71), 0),
    }


def left_panel(tiles, index, count):
    live = (jnp.arange(KA) < count[:, None]).astype(jnp.float32)
    onehot = (index[:, :, None] == jnp.arange(MB * W)[None, None, :]).astype(jnp.float32) * live[:, :, None]
    dense = jnp.einsum('rap,rauv->rpuv', onehot, tiles.astype(jnp.float32), precision=lax.Precision.HIGHEST)
    dense = dense.reshape(N_ROW, MB, W, TILE, TILE).transpose(0, 1, 3, 2, 4)
    return dense.reshape(ROWS, W * TILE)


def right_panel(tiles, index, count):
    live = (jnp.arange(KB) < count[:, None]).astype(jnp.float32)
    onehot = (index[:, :, None] == jnp.arange(W * NB)[None, None, :]).astype(jnp.float32) * live[:, :, None]
    dense = jnp.einsum('cbp,cbuv->cpuv', onehot, tiles.astype(jnp.float32), precision=lax.Precision.HIGHEST)
    dense = dense.reshape(N_COL, W, NB, TILE, TILE).transpose(1, 3, 0, 2, 4)
    return dense.reshape(W * TILE, COLS)


def reference(a_tiles, a_index, a_count, b_tiles, b_index, b_count, c_partial, prune_mask):
    expanded = c_partial
    for section in range(SECTIONS):
        left = left_panel(a_tiles[:, N_COL - 1, section], a_index[:, N_COL - 1, section], a_count[:, N_COL - 1, section])
        right = right_panel(b_tiles[N_ROW - 2 + section], b_index[N_ROW - 2 + section], b_count[N_ROW - 2 + section])
        expanded = expanded + jnp.dot(left, right, precision=lax.Precision.HIGHEST)
    keep = jnp.repeat(jnp.repeat(prune_mask.astype(jnp.float32), TILE, axis=0), TILE, axis=1)
    kept = expanded * expanded * keep
    colsum = jnp.sum(kept, axis=0)
    return kept * (ROWS / colsum)[None, :]
```

```python
import jax
import jax.numpy as jnp
from jax import lax
from jax.experimental import pallas as pl
from jax.experimental.pallas import tpu as pltpu
from jax.sharding import PartitionSpec as P

MB = 4
NB = 4
W = 32
KA = 16
KB = 16
SECTIONS = 2
TILE = 128
ROWS = 16384
Y_LO, Z, CORE = 2, 8, 2
Y_HI, X = 4, 4
N_ROW, N_COL = Y_LO * Z * CORE, Y_HI * X
LQ = SECTIONS * KA // X
RQ = KB // Z
PAD = 16


def row_of(y_lo, z, core):
    return (y_lo * Z + z) * CORE + core


def col_of(y_hi, x):
    return y_hi * X + x


def flat(row, col):
    return row * N_COL + col


def messages(tiles, slots, parts):
    per = tiles.shape[0] // parts
    body = tiles.reshape(parts, per * TILE, TILE)
    tail = jnp.pad(slots.astype(jnp.bfloat16).reshape(parts, 1, per), ((0, 0), (0, PAD - 1), (0, TILE - per)))
    return jnp.concatenate([body, tail], axis=1)


def slots_of(got, per):
    return got[:, per * TILE, :per].astype(jnp.int32).reshape(-1)


def only(condition, array):
    return jnp.where(condition, array, jnp.zeros_like(array))


X_GROUPS = [[col_of(y, x) for x in range(X)] for y in range(Y_HI)]
Z_GROUPS = [[row_of(y, z, c) for z in range(Z)] for y in range(Y_LO) for c in range(CORE)]
CY_GROUPS = [[row_of(y, z, c) for y in range(Y_LO) for c in range(CORE)] for z in range(Z)]


def gather(array, axis, groups):
    n = len(groups[0])
    return lax.all_to_all(jnp.broadcast_to(array, (n,) + array.shape), axis, 0, 0, axis_index_groups=groups)


def left_everywhere(message, row, col):
    y_lo, y_hi, x = row // (Z * CORE), col // X, col % X
    last = y_hi == Y_HI - 1
    have = only(last & (x == X - 1), message[X - 1])
    for q in (1, 0, 2):
        pairs = [(col_of(Y_HI - 1, X - 1), col_of(Y_HI - 1, q))]
        have = have + lax.ppermute(message[q], "col", pairs)
    both = ("row", "col")
    first, second = [], []
    for x_ in range(X):
        for z in range(Z):
            for c in range(CORE):
                lo, hi = row_of(0, z, c), row_of(1, z, c)
                at = lambda r, y: flat(r, col_of(y, x_))
                first += [(at(lo, 3), at(lo, 0)), (at(hi, 3), at(hi, 2))]
                second += [(at(lo, 3), at(lo, 2)), (at(lo, 0), at(lo, 1)), (at(hi, 3), at(hi, 0)), (at(hi, 2), at(hi, 1))]
    have = have + lax.ppermute(have, both, first)
    have = have + lax.ppermute(have, both, second)
    return gather(have, "col", X_GROUPS)


def right_everywhere(message, row):
    y_lo, z = row // (Z * CORE), (row // CORE) % Z
    have = only((y_lo == Y_LO - 1) & (z == Z - 1), message[Z - 1])
    for q in (3, 2, 4, 1, 5, 0, 6):
        pairs = [(row_of(1, Z - 1, c), row_of(1, q, c)) for c in range(CORE)]
        have = have + lax.ppermute(message[q], "row", pairs)
    have = have + lax.ppermute(have, "row", [(row_of(1, z_, c), row_of(0, z_, c)) for z_ in range(Z) for c in range(CORE)])
    mine = gather(have, "row", Z_GROUPS)
    other = lax.ppermute(mine, "row", [(r, r ^ 1) for r in range(N_ROW)])
    return mine, other


def product_kernel(core_ref, place_ref, block_ref, mask_ref, left_ref, mine_ref, other_ref, c_ref, kept_ref, sum_ref):
    kept_ref[...] = c_ref[...]
    core = core_ref[0]

    def section(base, right_ref):
        def step(t, carry):
            a = base + t
            quarter, inside = a // LQ, a % LQ
            rows = pl.ds(pl.multiple_of(block_ref[a] * TILE, TILE), TILE)
            for n in range(NB):
                p = place_ref[a * NB + n]

                @pl.when(p >= 0)
                def _():
                    left = left_ref[quarter, pl.ds(pl.multiple_of(inside * TILE, TILE), TILE), :]
                    right = right_ref[p // RQ, pl.ds(pl.multiple_of((p % RQ) * TILE, TILE), TILE), :]
                    columns = pl.ds(n * TILE, TILE)
                    kept_ref[rows, columns] += jnp.dot(left, right, preferred_element_type=jnp.float32)

            return carry

        lax.fori_loop(0, KA, step, 0)

    section(core * KA, mine_ref)
    section((1 - core) * KA, other_ref)
    for n in range(NB):
        columns = pl.ds(n * TILE, TILE)
        total = jnp.zeros((1, TILE), jnp.float32)
        for m in range(MB):
            rows = pl.ds(m * TILE, TILE)
            value = kept_ref[rows, columns]
            value = value * value * mask_ref[m * NB + n].astype(jnp.float32)
            kept_ref[rows, columns] = value
            total = total + jnp.sum(value, axis=0, keepdims=True)
        sum_ref[:, columns] = total


def product(core, place, block, mask, left, mine, other, c_partial):
    smem = pl.BlockSpec(memory_space=pltpu.SMEM)
    vmem = pl.BlockSpec(memory_space=pltpu.VMEM)
    return pl.pallas_call(
        product_kernel,
        out_shape=(
            jax.ShapeDtypeStruct((MB * TILE, NB * TILE), jnp.float32),
            jax.ShapeDtypeStruct((1, NB * TILE), jnp.float32),
        ),
        in_specs=[smem] * 4 + [vmem] * 4,
        out_specs=(vmem, vmem),
        compiler_params=pltpu.CompilerParams(vmem_limit_bytes=12 * 1024 * 1024),
    )(core, place, block, mask, left, mine, other, c_partial)


def local(a_tiles, a_index, a_count, b_tiles, b_index, b_count, c_partial, prune_mask):
    row, col = lax.axis_index("row"), lax.axis_index("col")
    core = row % CORE
    left_slots = jnp.where(jnp.arange(KA)[None, :] < a_count[0, 0][:, None], a_index[0, 0], -1)
    right_slots = jnp.where(jnp.arange(KB) < b_count[0, 0], b_index[0, 0], -1)
    left = left_everywhere(messages(a_tiles.reshape(SECTIONS * KA, TILE, TILE), left_slots, X), row, col)
    mine, other = right_everywhere(messages(b_tiles.reshape(KB, TILE, TILE), right_slots, Z), row)
    slot = slots_of(left, LQ)
    slot_mine, slot_other = slots_of(mine, RQ), slots_of(other, RQ)
    section = jnp.arange(SECTIONS * KA) // KA
    facing = jnp.where((section == core)[:, None], slot_mine[None, :], slot_other[None, :])
    wanted = (slot % W)[:, None] * NB + jnp.arange(NB)[None, :]
    hit = (facing[:, None, :] == wanted[:, :, None]) & (slot >= 0)[:, None, None]
    place = jnp.max(jnp.where(hit, jnp.arange(KB)[None, None, :], -1), axis=2).reshape(-1)
    block = jnp.maximum(slot, 0) // W
    kept, partial = product(core.reshape(1), place, block, prune_mask.reshape(-1), left, mine, other, c_partial)
    total = jnp.sum(gather(partial[0], "row", CY_GROUPS), axis=0)
    total = jnp.sum(gather(total, "row", Z_GROUPS), axis=0)
    return kept * (ROWS / total)[None, :]


def solution(mesh):
    return jax.shard_map(
        local,
        mesh=mesh,
        in_specs=(
            P("row", "col", None, None, None, None),
            P("row", "col", None, None),
            P("row", "col", None),
            P("row", "col", None, None, None),
            P("row", "col", None),
            P("row", "col"),
            P("row", "col"),
            P("row", "col"),
        ),
        out_specs=P("row", "col"),
        check_vma=False,
    )
```

```python
import jax
import jax.numpy as jnp
from jax import lax
from jax.experimental import pallas as pl
from jax.experimental.pallas import tpu as pltpu
from jax.sharding import PartitionSpec as P

MB = 4
NB = 4
W = 32
KA = 16
KB = 16
SECTIONS = 2
TILE = 128
ROWS = 16384
Y_LO, Z, CORE = 2, 8, 2
Y_HI, X = 4, 4
N_ROW, N_COL = Y_LO * Z * CORE, Y_HI * X
LQ = SECTIONS * KA // X
HALVES = 2
RH = KB // HALVES
PAD = 16


def row_of(y_lo, z, core):
    return (y_lo * Z + z) * CORE + core


def col_of(y_hi, x):
    return y_hi * X + x


def flat(row, col):
    return row * N_COL + col


def slots_of(got, per):
    return got[:, per * TILE, :per].astype(jnp.int32).reshape(-1)


Z_GROUPS = [[row_of(y, z, c) for z in range(Z)] for y in range(Y_LO) for c in range(CORE)]
CY_GROUPS = [[row_of(y, z, c) for y in range(Y_LO) for c in range(CORE)] for z in range(Z)]


def gather(array, axis, groups):
    n = len(groups[0])
    return lax.all_to_all(jnp.broadcast_to(array, (n,) + array.shape), axis, 0, 0, axis_index_groups=groups)


def y_pairs():
    first, second = [], []
    for z in range(Z):
        for c in range(CORE):
            for x in range(X):
                lo = lambda y: flat(row_of(0, z, c), col_of(y, x))
                hi = lambda y: flat(row_of(1, z, c), col_of(y, x))
                first += [(lo(3), lo(0)), (hi(3), hi(2))]
                second += [(lo(3), lo(2)), (lo(0), lo(1)), (hi(3), hi(0)), (hi(2), hi(1))]
    return first, second


def after(array, *others):
    return lax.optimization_barrier((array, *others))[0]


def messages_kernel(a_index_ref, a_count_ref, b_index_ref, b_count_ref, a_ref, b_ref, *refs):
    quarter_refs, left_ref, half_refs, sems = refs[: X - 1], refs[X - 1], refs[X : X + HALVES], refs[-1]
    row, col = lax.axis_index("row"), lax.axis_index("col")
    own, root = col == N_COL - 1, row >= N_ROW - CORE
    lane = lax.broadcasted_iota(jnp.int32, (PAD, TILE), 1)
    body, end = pl.ds(0, LQ * TILE), pl.ds(LQ * TILE, PAD)

    def tail(slot_of):
        line = jnp.full((PAD, TILE), -1, jnp.int32)
        for t in range(LQ):
            line = jnp.where(lane == t, slot_of(t), line)
        return line.astype(jnp.float32).astype(jnp.bfloat16)

    @pl.when(own)
    def _():
        outs = (*quarter_refs, left_ref)
        copies = [
            pltpu.make_async_copy(a_ref.at[pl.ds(q * LQ * TILE, LQ * TILE), :], ref.at[body, :], sems.at[q])
            for q, ref in enumerate(outs)
        ]
        for copy in copies:
            copy.start()
        for q, ref in enumerate(outs):

            def slot_of(t, q=q):
                section, place = divmod(q * LQ + t, KA)
                return jnp.where(place < a_count_ref[section], a_index_ref[section * KA + place], -1)

            ref[end, :] = tail(slot_of)
        for copy in copies:
            copy.wait()

    @pl.when(jnp.logical_not(own))
    def _():
        left_ref[...] = jnp.zeros_like(left_ref)

    @pl.when(root)
    def _():
        copies = [
            pltpu.make_async_copy(b_ref.at[pl.ds(h * RH * TILE, RH * TILE), :], ref.at[body, :], sems.at[X + h])
            for h, ref in enumerate(half_refs)
        ]
        for copy in copies:
            copy.start()
        for h, ref in enumerate(half_refs):

            def slot_of(t, h=h):
                return jnp.where(h * RH + t < b_count_ref[0], b_index_ref[h * RH + t], -1)

            ref[end, :] = tail(slot_of)
        for copy in copies:
            copy.wait()

    @pl.when(jnp.logical_not(root))
    def _():
        for ref in half_refs:
            ref[...] = jnp.zeros_like(ref)


def messages(a_tiles, a_index, a_count, b_tiles, b_index, b_count):
    smem = pl.BlockSpec(memory_space=pltpu.SMEM)
    vmem = pl.BlockSpec(memory_space=pltpu.VMEM)
    hbm = pl.BlockSpec(memory_space=pltpu.HBM)
    return pl.pallas_call(
        messages_kernel,
        out_shape=[jax.ShapeDtypeStruct((LQ * TILE + PAD, TILE), jnp.bfloat16)] * (X + HALVES),
        in_specs=[smem] * 4 + [hbm] * 2,
        out_specs=[vmem] * (X + HALVES),
        scratch_shapes=[pltpu.SemaphoreType.DMA((X + HALVES,))],
        compiler_params=pltpu.CompilerParams(vmem_limit_bytes=4 * 1024 * 1024),
    )(a_index, a_count, b_index, b_count, a_tiles, b_tiles)


def right_steps(h):
    def at(place):
        return (Z - 1 + (place if h == 0 else -place)) % Z

    along = ([(0, 3)], [(0, 2), (3, 5)], [(2, 1), (0, 7), (3, 4), (5, 6)])
    return [[((1, Z - 1), (0, Z - 1))]] + [[((y, at(a)), (y, at(b))) for a, b in step for y in range(Y_LO)] for step in along]


def panels_everywhere(a_tiles, a_index, a_count, b_tiles, b_index, b_count, c_partial):
    both = ("row", "col")
    first, second = y_pairs()
    *quarters, left, half0, half1 = messages(
        a_tiles.reshape(SECTIONS * KA * TILE, TILE),
        a_index.reshape(-1),
        a_count.reshape(-1),
        b_tiles.reshape(KB * TILE, TILE),
        b_index.reshape(-1),
        b_count.reshape(-1),
    )
    mine = [half0, half1]
    for q in (1, 0, 2):
        with jax.named_scope("left_scatter"):
            left = left + lax.ppermute(quarters[q], "col", [(col_of(Y_HI - 1, X - 1), col_of(Y_HI - 1, q))])

    def right_step(i):
        for h in range(HALVES):
            with jax.named_scope("right_step"):
                pairs = [(row_of(*a, c), row_of(*b, c)) for a, b in right_steps(h)[i] for c in range(CORE)]
                mine[h] = mine[h] + lax.ppermute(mine[h], "row", pairs)

    def right_after(*arrays):
        for h in range(HALVES):
            mine[h] = after(mine[h], *arrays)

    right_step(0)
    c_partial = after(c_partial, left)
    right_after(left)
    with jax.named_scope("left_y"):
        left = left + lax.ppermute(left, both, first)
    right_step(1)
    held = hold(c_partial)
    right_after(left, held)
    with jax.named_scope("left_y"):
        left = left + lax.ppermute(left, both, second)
    right_step(2)
    right_after(left)
    lefts = [left]
    for d in range(1, X):
        with jax.named_scope("left_x"):
            pairs = [(col_of(y, x_), col_of(y, (x_ + d) % X)) for y in range(Y_HI) for x_ in range(X)]
            lefts.append(lax.ppermute(left, "col", pairs))
    right_step(3)
    with jax.named_scope("right_core"):
        other = lax.ppermute(jnp.stack(mine), "row", [(r, r ^ 1) for r in range(N_ROW)])
    return lefts, [*mine, other], held


def hold_kernel(c_ref, held_ref):
    held_ref[...] = c_ref[...]


def hold(c_partial):
    vmem = pl.BlockSpec(memory_space=pltpu.VMEM)
    return pl.pallas_call(
        hold_kernel,
        out_shape=jax.ShapeDtypeStruct((MB * TILE, NB * TILE), jnp.float32),
        in_specs=[vmem],
        out_specs=vmem,
        compiler_params=pltpu.CompilerParams(vmem_limit_bytes=4 * 1024 * 1024),
    )(c_partial)


def product_kernel(slot_ref, table_ref, mask_ref, *refs):
    lefts, (*mine, other_ref), (held_ref, kept_ref, sum_ref) = refs[:X], refs[X : X + HALVES + 1], refs[X + HALVES + 1 :]
    rights = [*mine, *(other_ref.at[h] for h in range(HALVES))]
    kept_ref[...] = held_ref[...]
    core, x = lax.axis_index("row") % CORE, lax.axis_index("col") % X
    for d, left_ref in enumerate(lefts):
        section = ((x + X - d) % X) // (X // SECTIONS)
        which = jnp.where(section == core, 0, 1)

        def step(t, carry):
            slot = slot_ref[d * LQ + t]

            @pl.when(slot >= 0)
            def _():
                rows = pl.ds(pl.multiple_of((slot // W) * TILE, TILE), TILE)
                tile = pl.ds(pl.multiple_of(t * TILE, TILE), TILE)
                for n in range(NB):
                    p = table_ref[which * W * NB + (slot % W) * NB + n]

                    @pl.when(p >= 0)
                    def _():
                        for r in range(2 * HALVES):

                            @pl.when(which * HALVES + p // RH == r)
                            def _():
                                right = rights[r][pl.ds(pl.multiple_of((p % RH) * TILE, TILE), TILE), :]
                                columns = pl.ds(n * TILE, TILE)
                                kept_ref[rows, columns] += jnp.dot(
                                    left_ref[tile, :], right, preferred_element_type=jnp.float32
                                )

            return carry

        lax.fori_loop(0, LQ, step, 0)

    for n in range(NB):
        columns = pl.ds(n * TILE, TILE)
        total = jnp.zeros((1, TILE), jnp.float32)
        for m in range(MB):
            rows = pl.ds(m * TILE, TILE)
            value = kept_ref[rows, columns]
            value = value * value * mask_ref[m * NB + n].astype(jnp.float32)
            kept_ref[rows, columns] = value
            total = total + jnp.sum(value, axis=0, keepdims=True)
        sum_ref[:, columns] = total


def product(slot, table, mask, lefts, rights, held):
    smem = pl.BlockSpec(memory_space=pltpu.SMEM)
    vmem = pl.BlockSpec(memory_space=pltpu.VMEM)
    return pl.pallas_call(
        product_kernel,
        out_shape=(
            jax.ShapeDtypeStruct((MB * TILE, NB * TILE), jnp.float32),
            jax.ShapeDtypeStruct((1, NB * TILE), jnp.float32),
        ),
        in_specs=[smem] * 3 + [vmem] * (len(lefts) + len(rights) + 1),
        out_specs=(vmem, vmem),
        input_output_aliases={3 + len(lefts) + len(rights): 0},
        compiler_params=pltpu.CompilerParams(vmem_limit_bytes=6 * 1024 * 1024),
    )(slot, table, mask, *lefts, *rights, held)


def local(a_tiles, a_index, a_count, b_tiles, b_index, b_count, c_partial, prune_mask):
    lefts, rights, held = panels_everywhere(a_tiles, a_index, a_count, b_tiles, b_index, b_count, c_partial)
    *mine, other = rights
    facing = jnp.stack([slots_of(right[None], RH) for right in (*mine, *other)]).reshape(2, 1, KB)
    hit = facing == jnp.arange(W * NB)[None, :, None]
    table = jnp.max(jnp.where(hit, jnp.arange(KB)[None, None, :], -1), axis=2).reshape(-1)
    slot = jnp.stack([slots_of(left[None], LQ) for left in lefts]).reshape(-1)
    kept, partial = product(slot, table, prune_mask.reshape(-1), lefts, rights, held)
    total = jnp.sum(gather(partial[0], "row", CY_GROUPS), axis=0)
    total = jnp.sum(gather(total, "row", Z_GROUPS), axis=0)
    return kept * (ROWS / total)[None, :]


def solution(mesh):
    return jax.shard_map(
        local,
        mesh=mesh,
        in_specs=(
            P("row", "col", None, None, None, None),
            P("row", "col", None, None),
            P("row", "col", None),
            P("row", "col", None, None, None),
            P("row", "col", None),
            P("row", "col"),
            P("row", "col"),
            P("row", "col"),
        ),
        out_specs=P("row", "col"),
        check_vma=False,
    )
```

```python
import jax
import jax.numpy as jnp
from jax import lax
from jax.experimental import pallas as pl
from jax.experimental.pallas import tpu as pltpu
from jax.sharding import PartitionSpec as P

MB = 4
NB = 4
W = 32
KA = 16
KB = 16
SECTIONS = 2
TILE = 128
ROWS = 16384
Y_LO, Z, CORE = 2, 8, 2
Y_HI, X = 4, 4
N_ROW, N_COL = Y_LO * Z * CORE, Y_HI * X
LQ = SECTIONS * KA // X
HALVES = 2
RH = KB // HALVES
PAD = 16


def row_of(y_lo, z, core):
    return (y_lo * Z + z) * CORE + core


def col_of(y_hi, x):
    return y_hi * X + x


def flat(row, col):
    return row * N_COL + col


def slots_of(got, per):
    return got[:, per * TILE, :per].astype(jnp.int32).reshape(-1)


Z_GROUPS = [[row_of(y, z, c) for z in range(Z)] for y in range(Y_LO) for c in range(CORE)]
CY_GROUPS = [[row_of(y, z, c) for y in range(Y_LO) for c in range(CORE)] for z in range(Z)]


def gather(array, axis, groups):
    n = len(groups[0])
    return lax.all_to_all(jnp.broadcast_to(array, (n,) + array.shape), axis, 0, 0, axis_index_groups=groups)


def y_pairs():
    first, second = [], []
    for z in range(Z):
        for c in range(CORE):
            for x in range(X):
                lo = lambda y: flat(row_of(0, z, c), col_of(y, x))
                hi = lambda y: flat(row_of(1, z, c), col_of(y, x))
                first += [(lo(3), lo(0)), (hi(3), hi(2))]
                second += [(lo(3), lo(2)), (lo(0), lo(1)), (hi(3), hi(0)), (hi(2), hi(1))]
    return first, second


def after(array, *others):
    return lax.optimization_barrier((array, *others))[0]


def messages_kernel(a_index_ref, a_count_ref, b_index_ref, b_count_ref, a_ref, b_ref, *refs):
    *quarter_refs, left_ref, right_ref, sems = refs
    half_refs = [right_ref.at[h] for h in range(HALVES)]
    row, col = lax.axis_index("row"), lax.axis_index("col")
    own, root = col == N_COL - 1, row >= N_ROW - CORE
    lane = lax.broadcasted_iota(jnp.int32, (PAD, TILE), 1)
    body, end = pl.ds(0, LQ * TILE), pl.ds(LQ * TILE, PAD)

    def tail(slot_of):
        line = jnp.full((PAD, TILE), -1, jnp.int32)
        for t in range(LQ):
            line = jnp.where(lane == t, slot_of(t), line)
        return line.astype(jnp.float32).astype(jnp.bfloat16)

    @pl.when(own)
    def _():
        outs = (*quarter_refs, left_ref)
        copies = [
            pltpu.make_async_copy(a_ref.at[pl.ds(q * LQ * TILE, LQ * TILE), :], ref.at[body, :], sems.at[q])
            for q, ref in enumerate(outs)
        ]
        for copy in copies:
            copy.start()
        for q, ref in enumerate(outs):

            def slot_of(t, q=q):
                section, place = divmod(q * LQ + t, KA)
                return jnp.where(place < a_count_ref[section], a_index_ref[section * KA + place], -1)

            ref[end, :] = tail(slot_of)
        for copy in copies:
            copy.wait()

    @pl.when(jnp.logical_not(own))
    def _():
        left_ref[...] = jnp.zeros_like(left_ref)

    @pl.when(root)
    def _():
        copies = [
            pltpu.make_async_copy(b_ref.at[pl.ds(h * RH * TILE, RH * TILE), :], ref.at[body, :], sems.at[X + h])
            for h, ref in enumerate(half_refs)
        ]
        for copy in copies:
            copy.start()
        for h, ref in enumerate(half_refs):

            def slot_of(t, h=h):
                return jnp.where(h * RH + t < b_count_ref[0], b_index_ref[h * RH + t], -1)

            ref[end, :] = tail(slot_of)
        for copy in copies:
            copy.wait()

    @pl.when(jnp.logical_not(root))
    def _():
        right_ref[...] = jnp.zeros_like(right_ref)


def messages(a_tiles, a_index, a_count, b_tiles, b_index, b_count):
    smem = pl.BlockSpec(memory_space=pltpu.SMEM)
    vmem = pl.BlockSpec(memory_space=pltpu.VMEM)
    hbm = pl.BlockSpec(memory_space=pltpu.HBM)
    return pl.pallas_call(
        messages_kernel,
        out_shape=[jax.ShapeDtypeStruct((LQ * TILE + PAD, TILE), jnp.bfloat16)] * X
        + [jax.ShapeDtypeStruct((HALVES, RH * TILE + PAD, TILE), jnp.bfloat16)],
        in_specs=[smem] * 4 + [hbm] * 2,
        out_specs=[vmem] * (X + 1),
        scratch_shapes=[pltpu.SemaphoreType.DMA((X + HALVES,))],
        compiler_params=pltpu.CompilerParams(vmem_limit_bytes=4 * 1024 * 1024),
    )(a_index, a_count, b_index, b_count, a_tiles, b_tiles)


def right_steps(h):
    def pairs(*moves):
        def at(y, place):
            return y, (Z - 1 + (place if h == 0 else -place)) % Z

        return [(at(y, a), at(to, b)) for y, a, to, b in moves]

    both = [(y, a, y, b) for a, b in ((2, 1), (0, 7), (3, 4), (5, 6)) for y in range(Y_LO)]
    return [
        [pairs((1, 0, 1, 3))],
        [pairs((1, 0, 1, 2), (1, 3, 1, 5), (0, 0, 0, 2)), pairs((1, 3, 0, 3), (0, 0, 0, 5))],
        [pairs(*both)],
    ]


def panels_everywhere(a_tiles, a_index, a_count, b_tiles, b_index, b_count, c_partial):
    both = ("row", "col")
    first, second = y_pairs()
    *quarters, left, right = messages(
        a_tiles.reshape(SECTIONS * KA * TILE, TILE),
        a_index.reshape(-1),
        a_count.reshape(-1),
        b_tiles.reshape(KB * TILE, TILE),
        b_index.reshape(-1),
        b_count.reshape(-1),
    )
    for q in (1, 0, 2):
        with jax.named_scope("left_scatter"):
            left = left + lax.ppermute(quarters[q], "col", [(col_of(Y_HI - 1, X - 1), col_of(Y_HI - 1, q))])

    def right_send(array, pairs):
        with jax.named_scope("right_step"):
            return lax.ppermute(array, "row", [(row_of(*a, c), row_of(*b, c)) for a, b in pairs for c in range(CORE)])

    def right_step(array, ops):
        return sum([right_send(array, pairs) for pairs in ops], array)

    along = [right_send(right[h], right_steps(h)[0][0]) for h in range(HALVES)]
    right = right_step(right, [[((1, Z - 1), (0, Z - 1))]])
    mine = [after(right[h] + along[h], left) for h in range(HALVES)]
    c_partial = after(c_partial, left)
    with jax.named_scope("left_y"):
        left = left + lax.ppermute(left, both, first)
    mine = [right_step(mine[h], right_steps(h)[1]) for h in range(HALVES)]
    held = hold(c_partial)
    mine = [after(half, left, held) for half in mine]
    with jax.named_scope("left_y"):
        left = left + lax.ppermute(left, both, second)
    mine = [right_step(mine[h], right_steps(h)[2]) for h in range(HALVES)]
    mine = [after(half, left) for half in mine]
    lefts = [left]
    for d in range(1, X):
        with jax.named_scope("left_x"):
            pairs = [(col_of(y, x_), col_of(y, (x_ + d) % X)) for y in range(Y_HI) for x_ in range(X)]
            lefts.append(lax.ppermute(left, "col", pairs))
    with jax.named_scope("right_core"):
        other = lax.ppermute(jnp.stack(mine), "row", [(r, r ^ 1) for r in range(N_ROW)])
    return lefts, [*mine, other], held


def hold_kernel(c_ref, held_ref):
    held_ref[...] = c_ref[...]


def hold(c_partial):
    vmem = pl.BlockSpec(memory_space=pltpu.VMEM)
    return pl.pallas_call(
        hold_kernel,
        out_shape=jax.ShapeDtypeStruct((MB * TILE, NB * TILE), jnp.float32),
        in_specs=[vmem],
        out_specs=vmem,
        compiler_params=pltpu.CompilerParams(vmem_limit_bytes=4 * 1024 * 1024),
    )(c_partial)


def product_kernel(slot_ref, table_ref, mask_ref, *refs):
    lefts, (*mine, other_ref), (held_ref, kept_ref, sum_ref) = refs[:X], refs[X : X + HALVES + 1], refs[X + HALVES + 1 :]
    rights = [*mine, *(other_ref.at[h] for h in range(HALVES))]
    kept_ref[...] = held_ref[...]
    core, x = lax.axis_index("row") % CORE, lax.axis_index("col") % X
    for d, left_ref in enumerate(lefts):
        section = ((x + X - d) % X) // (X // SECTIONS)
        which = jnp.where(section == core, 0, 1)

        def step(t, carry):
            slot = slot_ref[d * LQ + t]

            @pl.when(slot >= 0)
            def _():
                rows = pl.ds(pl.multiple_of((slot // W) * TILE, TILE), TILE)
                tile = pl.ds(pl.multiple_of(t * TILE, TILE), TILE)
                for n in range(NB):
                    p = table_ref[which * W * NB + (slot % W) * NB + n]

                    @pl.when(p >= 0)
                    def _():
                        for r in range(2 * HALVES):

                            @pl.when(which * HALVES + p // RH == r)
                            def _():
                                right = rights[r][pl.ds(pl.multiple_of((p % RH) * TILE, TILE), TILE), :]
                                columns = pl.ds(n * TILE, TILE)
                                kept_ref[rows, columns] += jnp.dot(
                                    left_ref[tile, :], right, preferred_element_type=jnp.float32
                                )

            return carry

        lax.fori_loop(0, LQ, step, 0)

    for n in range(NB):
        columns = pl.ds(n * TILE, TILE)
        total = jnp.zeros((1, TILE), jnp.float32)
        for m in range(MB):
            rows = pl.ds(m * TILE, TILE)
            value = kept_ref[rows, columns]
            value = value * value * mask_ref[m * NB + n].astype(jnp.float32)
            kept_ref[rows, columns] = value
            total = total + jnp.sum(value, axis=0, keepdims=True)
        sum_ref[:, columns] = total


def product(slot, table, mask, lefts, rights, held):
    smem = pl.BlockSpec(memory_space=pltpu.SMEM)
    vmem = pl.BlockSpec(memory_space=pltpu.VMEM)
    return pl.pallas_call(
        product_kernel,
        out_shape=(
            jax.ShapeDtypeStruct((MB * TILE, NB * TILE), jnp.float32),
            jax.ShapeDtypeStruct((1, NB * TILE), jnp.float32),
        ),
        in_specs=[smem] * 3 + [vmem] * (len(lefts) + len(rights) + 1),
        out_specs=(vmem, vmem),
        input_output_aliases={3 + len(lefts) + len(rights): 0},
        compiler_params=pltpu.CompilerParams(vmem_limit_bytes=6 * 1024 * 1024),
    )(slot, table, mask, *lefts, *rights, held)


def local(a_tiles, a_index, a_count, b_tiles, b_index, b_count, c_partial, prune_mask):
    lefts, rights, held = panels_everywhere(a_tiles, a_index, a_count, b_tiles, b_index, b_count, c_partial)
    *mine, other = rights
    facing = jnp.stack([slots_of(right[None], RH) for right in (*mine, *other)]).reshape(2, 1, KB)
    hit = facing == jnp.arange(W * NB)[None, :, None]
    table = jnp.max(jnp.where(hit, jnp.arange(KB)[None, None, :], -1), axis=2).reshape(-1)
    slot = jnp.stack([slots_of(left[None], LQ) for left in lefts]).reshape(-1)
    kept, partial = product(slot, table, prune_mask.reshape(-1), lefts, rights, held)
    total = jnp.sum(gather(partial[0], "row", CY_GROUPS), axis=0)
    total = jnp.sum(gather(total, "row", Z_GROUPS), axis=0)
    return kept * (ROWS / total)[None, :]


def solution(mesh):
    return jax.shard_map(
        local,
        mesh=mesh,
        in_specs=(
            P("row", "col", None, None, None, None),
            P("row", "col", None, None),
            P("row", "col", None),
            P("row", "col", None, None, None),
            P("row", "col", None),
            P("row", "col"),
            P("row", "col"),
            P("row", "col"),
        ),
        out_specs=P("row", "col"),
        check_vma=False,
    )
```

```python
import jax
import jax.numpy as jnp
from jax import lax
from jax.experimental import pallas as pl
from jax.experimental.pallas import tpu as pltpu
from jax.sharding import PartitionSpec as P

MB = 4
NB = 4
W = 32
KA = 16
KB = 16
SECTIONS = 2
TILE = 128
ROWS = 16384
Y_LO, Z, CORE = 2, 8, 2
Y_HI, X = 4, 4
N_ROW, N_COL = Y_LO * Z * CORE, Y_HI * X
LQ = SECTIONS * KA // X
HALVES = 2
RH = KB // HALVES
PAD = 16


def row_of(y_lo, z, core):
    return (y_lo * Z + z) * CORE + core


def col_of(y_hi, x):
    return y_hi * X + x


def flat(row, col):
    return row * N_COL + col


def slots_of(got, per):
    return got[:, per * TILE, :per].astype(jnp.int32).reshape(-1)


Z_GROUPS = [[row_of(y, z, c) for z in range(Z)] for y in range(Y_LO) for c in range(CORE)]
CY_GROUPS = [[row_of(y, z, c) for y in range(Y_LO) for c in range(CORE)] for z in range(Z)]


def gather(array, axis, groups):
    n = len(groups[0])
    return lax.all_to_all(jnp.broadcast_to(array, (n,) + array.shape), axis, 0, 0, axis_index_groups=groups)


def y_pairs():
    first, second = [], []
    for z in range(Z):
        for c in range(CORE):
            for x in range(X):
                lo = lambda y: flat(row_of(0, z, c), col_of(y, x))
                hi = lambda y: flat(row_of(1, z, c), col_of(y, x))
                first += [(lo(3), lo(0)), (hi(3), hi(2))]
                second += [(lo(3), lo(2)), (lo(0), lo(1)), (hi(3), hi(0)), (hi(2), hi(1))]
    return first, second


def after(array, *others):
    return lax.optimization_barrier((array, *others))[0]


def fill(tiles_ref, message_refs, slot_of, sems):
    rows = RH * TILE
    lane = lax.broadcasted_iota(jnp.int32, (PAD, TILE), 1)
    copies = [
        pltpu.make_async_copy(tiles_ref.at[pl.ds(i * rows, rows), :], ref.at[pl.ds(0, rows), :], sems.at[i])
        for i, ref in enumerate(message_refs)
    ]
    for copy in copies:
        copy.start()
    for i, ref in enumerate(message_refs):
        line = jnp.full((PAD, TILE), -1, jnp.int32)
        for t in range(RH):
            line = jnp.where(lane == t, slot_of(i * RH + t), line)
        ref[pl.ds(rows, PAD), :] = line.astype(jnp.float32).astype(jnp.bfloat16)
    for copy in copies:
        copy.wait()


def left_kernel(index_ref, count_ref, tiles_ref, *refs):
    *quarter_refs, own_ref, sems = refs
    own = lax.axis_index("col") == N_COL - 1

    @pl.when(own)
    def _():
        def slot_of(i):
            section, place = divmod(i, KA)
            return jnp.where(place < count_ref[section], index_ref[section * KA + place], -1)

        fill(tiles_ref, (*quarter_refs, own_ref), slot_of, sems)

    @pl.when(jnp.logical_not(own))
    def _():
        own_ref[...] = jnp.zeros_like(own_ref)


def right_kernel(index_ref, count_ref, tiles_ref, right_ref, sems):
    root = lax.axis_index("row") >= N_ROW - CORE

    @pl.when(root)
    def _():
        def slot_of(i):
            return jnp.where(i < count_ref[0], index_ref[i], -1)

        fill(tiles_ref, [right_ref.at[h] for h in range(HALVES)], slot_of, sems)

    @pl.when(jnp.logical_not(root))
    def _():
        right_ref[...] = jnp.zeros_like(right_ref)


def messages(kernel, shapes, copies, index, count, tiles):
    smem = pl.BlockSpec(memory_space=pltpu.SMEM)
    return pl.pallas_call(
        kernel,
        out_shape=[jax.ShapeDtypeStruct(shape, jnp.bfloat16) for shape in shapes],
        in_specs=[smem, smem, pl.BlockSpec(memory_space=pl.ANY)],
        out_specs=[pl.BlockSpec(memory_space=pltpu.VMEM)] * len(shapes),
        scratch_shapes=[pltpu.SemaphoreType.DMA((copies,))],
        compiler_params=pltpu.CompilerParams(vmem_limit_bytes=4 * 1024 * 1024),
    )(index.reshape(-1), count.reshape(-1), tiles)


def right_steps(h):
    def pairs(*moves):
        def at(y, place):
            return y, (Z - 1 + (place if h == 0 else -place)) % Z

        return [(at(y, a), at(to, b)) for y, a, to, b in moves]

    both = [(y, a, y, b) for a, b in ((2, 1), (0, 7), (3, 4), (5, 6)) for y in range(Y_LO)]
    return [
        [pairs((1, 0, 1, 3))],
        [pairs((1, 0, 1, 2), (1, 3, 1, 5), (0, 0, 0, 2)), pairs((1, 3, 0, 3), (0, 0, 0, 5))],
        [pairs(*both)],
    ]


def panels_everywhere(a_tiles, a_index, a_count, b_tiles, b_index, b_count, c_partial):
    both = ("row", "col")
    first, second = y_pairs()
    message = (RH * TILE + PAD, TILE)
    a_tiles, b_tiles = a_tiles.reshape(SECTIONS * KA * TILE, TILE), b_tiles.reshape(KB * TILE, TILE)
    *quarters, left = messages(left_kernel, [message] * X, X, a_index, a_count, a_tiles)
    (right,) = messages(right_kernel, [(HALVES, *message)], HALVES, b_index, b_count, b_tiles)
    for q in (1, 0, 2):
        with jax.named_scope("left_scatter"):
            left = left + lax.ppermute(quarters[q], "col", [(col_of(Y_HI - 1, X - 1), col_of(Y_HI - 1, q))])

    def right_send(array, pairs):
        with jax.named_scope("right_step"):
            return lax.ppermute(array, "row", [(row_of(*a, c), row_of(*b, c)) for a, b in pairs for c in range(CORE)])

    def right_step(array, ops):
        return sum([right_send(array, pairs) for pairs in ops], array)

    along = [right_send(right[h], right_steps(h)[0][0]) for h in range(HALVES)]
    right = right_step(right, [[((1, Z - 1), (0, Z - 1))]])
    mine = [after(right[h] + along[h], left) for h in range(HALVES)]
    c_partial = after(c_partial, left)
    with jax.named_scope("left_y"):
        left = left + lax.ppermute(left, both, first)
    mine = [right_step(mine[h], right_steps(h)[1]) for h in range(HALVES)]
    held = hold(c_partial)
    mine = [after(half, left, held) for half in mine]
    with jax.named_scope("left_y"):
        left = left + lax.ppermute(left, both, second)
    mine = [right_step(mine[h], right_steps(h)[2]) for h in range(HALVES)]
    mine = [after(half, left) for half in mine]
    lefts = [left]
    for d in range(1, X):
        with jax.named_scope("left_x"):
            pairs = [(col_of(y, x_), col_of(y, (x_ + d) % X)) for y in range(Y_HI) for x_ in range(X)]
            lefts.append(lax.ppermute(left, "col", pairs))
    with jax.named_scope("right_core"):
        other = lax.ppermute(jnp.stack(mine), "row", [(r, r ^ 1) for r in range(N_ROW)])
    return lefts, [*mine, other], held


def hold_kernel(c_ref, held_ref):
    held_ref[...] = c_ref[...]


def hold(c_partial):
    vmem = pl.BlockSpec(memory_space=pltpu.VMEM)
    return pl.pallas_call(
        hold_kernel,
        out_shape=jax.ShapeDtypeStruct((MB * TILE, NB * TILE), jnp.float32),
        in_specs=[vmem],
        out_specs=vmem,
        compiler_params=pltpu.CompilerParams(vmem_limit_bytes=4 * 1024 * 1024),
    )(c_partial)


def product_kernel(slot_ref, table_ref, mask_ref, *refs):
    lefts, (*mine, other_ref), (held_ref, kept_ref, sum_ref) = refs[:X], refs[X : X + HALVES + 1], refs[X + HALVES + 1 :]
    rights = [*mine, *(other_ref.at[h] for h in range(HALVES))]
    kept_ref[...] = held_ref[...]
    core, x = lax.axis_index("row") % CORE, lax.axis_index("col") % X
    for d, left_ref in enumerate(lefts):
        section = ((x + X - d) % X) // (X // SECTIONS)
        which = jnp.where(section == core, 0, 1)

        def step(t, carry):
            slot = slot_ref[d * LQ + t]

            @pl.when(slot >= 0)
            def _():
                rows = pl.ds(pl.multiple_of((slot // W) * TILE, TILE), TILE)
                tile = pl.ds(pl.multiple_of(t * TILE, TILE), TILE)
                for n in range(NB):
                    p = table_ref[which * W * NB + (slot % W) * NB + n]

                    @pl.when(p >= 0)
                    def _():
                        for r in range(2 * HALVES):

                            @pl.when(which * HALVES + p // RH == r)
                            def _():
                                right = rights[r][pl.ds(pl.multiple_of((p % RH) * TILE, TILE), TILE), :]
                                columns = pl.ds(n * TILE, TILE)
                                kept_ref[rows, columns] += jnp.dot(
                                    left_ref[tile, :], right, preferred_element_type=jnp.float32
                                )

            return carry

        lax.fori_loop(0, LQ, step, 0)

    sum_ref[...] = jnp.zeros_like(sum_ref)
    for n in range(NB):
        columns = pl.ds(n * TILE, TILE)
        total = jnp.zeros((1, TILE), jnp.float32)
        for m in range(MB):
            rows = pl.ds(m * TILE, TILE)
            value = kept_ref[rows, columns]
            value = value * value * mask_ref[m * NB + n].astype(jnp.float32)
            kept_ref[rows, columns] = value
            total = total + jnp.sum(value, axis=0, keepdims=True)
        sum_ref[n : n + 1, :] = total


def product(slot, table, mask, lefts, rights, held):
    smem = pl.BlockSpec(memory_space=pltpu.SMEM)
    vmem = pl.BlockSpec(memory_space=pltpu.VMEM)
    return pl.pallas_call(
        product_kernel,
        out_shape=(
            jax.ShapeDtypeStruct((MB * TILE, NB * TILE), jnp.float32),
            jax.ShapeDtypeStruct((8, TILE), jnp.float32),
        ),
        in_specs=[smem] * 3 + [vmem] * (len(lefts) + len(rights) + 1),
        out_specs=(vmem, vmem),
        input_output_aliases={3 + len(lefts) + len(rights): 0},
        compiler_params=pltpu.CompilerParams(vmem_limit_bytes=6 * 1024 * 1024),
    )(slot, table, mask, *lefts, *rights, held)


def local(a_tiles, a_index, a_count, b_tiles, b_index, b_count, c_partial, prune_mask):
    lefts, rights, held = panels_everywhere(a_tiles, a_index, a_count, b_tiles, b_index, b_count, c_partial)
    *mine, other = rights
    facing = jnp.stack([slots_of(right[None], RH) for right in (*mine, *other)]).reshape(2, 1, KB)
    hit = facing == jnp.arange(W * NB)[None, :, None]
    table = jnp.max(jnp.where(hit, jnp.arange(KB)[None, None, :], -1), axis=2).reshape(-1)
    slot = jnp.stack([slots_of(left[None], LQ) for left in lefts]).reshape(-1)
    kept, partial = product(slot, table, prune_mask.reshape(-1), lefts, rights, held)
    total = jnp.sum(gather(partial, "row", CY_GROUPS), axis=0)
    total = jnp.sum(gather(total, "row", Z_GROUPS), axis=0)
    return kept * (ROWS / total[:NB]).reshape(1, NB * TILE)


def solution(mesh):
    return jax.shard_map(
        local,
        mesh=mesh,
        in_specs=(
            P("row", "col", None, None, None, None),
            P("row", "col", None, None),
            P("row", "col", None),
            P("row", "col", None, None, None),
            P("row", "col", None),
            P("row", "col"),
            P("row", "col"),
            P("row", "col"),
        ),
        out_specs=P("row", "col"),
        check_vma=False,
    )
```

```python
import jax
import jax.numpy as jnp
from jax import lax
from jax.experimental import pallas as pl
from jax.experimental.pallas import tpu as pltpu
from jax.sharding import PartitionSpec as P

MB = 4
NB = 4
W = 32
KA = 16
KB = 16
SECTIONS = 2
TILE = 128
ROWS = 16384
Y_LO, Z, CORE = 2, 8, 2
Y_HI, X = 4, 4
N_ROW, N_COL = Y_LO * Z * CORE, Y_HI * X
LQ = SECTIONS * KA // X
HALVES = 2
RH = KB // HALVES
PAD = 16


def row_of(y_lo, z, core):
    return (y_lo * Z + z) * CORE + core


def col_of(y_hi, x):
    return y_hi * X + x


def flat(row, col):
    return row * N_COL + col


def slots_of(got, per):
    return got[:, per * TILE, :per].astype(jnp.int32).reshape(-1)


Z_GROUPS = [[row_of(y, z, c) for z in range(Z)] for y in range(Y_LO) for c in range(CORE)]
CY_GROUPS = [[row_of(y, z, c) for y in range(Y_LO) for c in range(CORE)] for z in range(Z)]


def gather(array, axis, groups):
    n = len(groups[0])
    return lax.all_to_all(jnp.broadcast_to(array, (n,) + array.shape), axis, 0, 0, axis_index_groups=groups)


def y_pairs():
    first, second = [], []
    for z in range(Z):
        for c in range(CORE):
            for x in range(X):
                lo = lambda y: flat(row_of(0, z, c), col_of(y, x))
                hi = lambda y: flat(row_of(1, z, c), col_of(y, x))
                first += [(lo(3), lo(0)), (hi(3), hi(2))]
                second += [(lo(3), lo(2)), (lo(0), lo(1)), (hi(3), hi(0)), (hi(2), hi(1))]
    return first, second


def after(array, *others):
    return lax.optimization_barrier((array, *others))[0]


def fill(tiles_ref, message_refs, slot_of, sems):
    rows = RH * TILE
    lane = lax.broadcasted_iota(jnp.int32, (PAD, TILE), 1)
    copies = [
        pltpu.make_async_copy(tiles_ref.at[pl.ds(i * rows, rows), :], ref.at[pl.ds(0, rows), :], sems.at[i])
        for i, ref in enumerate(message_refs)
    ]
    for copy in copies:
        copy.start()
    for i, ref in enumerate(message_refs):
        line = jnp.full((PAD, TILE), -1, jnp.int32)
        for t in range(RH):
            line = jnp.where(lane == t, slot_of(i * RH + t), line)
        ref[pl.ds(rows, PAD), :] = line.astype(jnp.float32).astype(jnp.bfloat16)
    for copy in copies:
        copy.wait()


def left_kernel(index_ref, count_ref, tiles_ref, *refs):
    *quarter_refs, own_ref, sems = refs
    own = lax.axis_index("col") == N_COL - 1

    @pl.when(own)
    def _():
        def slot_of(i):
            section, place = divmod(i, KA)
            return jnp.where(place < count_ref[section], index_ref[section * KA + place], -1)

        fill(tiles_ref, (*quarter_refs, own_ref), slot_of, sems)

    @pl.when(jnp.logical_not(own))
    def _():
        own_ref[...] = jnp.zeros_like(own_ref)


def right_kernel(index_ref, count_ref, tiles_ref, right_ref, sems):
    root = lax.axis_index("row") >= N_ROW - CORE

    @pl.when(root)
    def _():
        def slot_of(i):
            return jnp.where(i < count_ref[0], index_ref[i], -1)

        fill(tiles_ref, [right_ref.at[h] for h in range(HALVES)], slot_of, sems)

    @pl.when(jnp.logical_not(root))
    def _():
        right_ref[...] = jnp.zeros_like(right_ref)


def messages(kernel, shapes, copies, index, count, tiles):
    smem = pl.BlockSpec(memory_space=pltpu.SMEM)
    return pl.pallas_call(
        kernel,
        out_shape=[jax.ShapeDtypeStruct(shape, jnp.bfloat16) for shape in shapes],
        in_specs=[smem, smem, pl.BlockSpec(memory_space=pl.ANY)],
        out_specs=[pl.BlockSpec(memory_space=pltpu.VMEM)] * len(shapes),
        scratch_shapes=[pltpu.SemaphoreType.DMA((copies,))],
        compiler_params=pltpu.CompilerParams(vmem_limit_bytes=4 * 1024 * 1024),
    )(index.reshape(-1), count.reshape(-1), tiles)


def right_steps(h):
    def pairs(*moves):
        def at(y, place):
            return y, (Z - 1 + (place if h == 0 else -place)) % Z

        return [(at(y, a), at(to, b)) for y, a, to, b in moves]

    both = [(y, a, y, b) for a, b in ((0, 1), (6, 7), (4, 5), (3, 2)) for y in range(Y_LO)]
    return [
        [pairs((1, 0, 1, 3))],
        [pairs((1, 0, 1, 6), (0, 0, 0, 6), (1, 3, 1, 4)), pairs((1, 3, 0, 3), (0, 0, 0, 4))],
        [pairs(*both)],
    ]


def panels_everywhere(a_tiles, a_index, a_count, b_tiles, b_index, b_count, c_partial):
    both = ("row", "col")
    first, second = y_pairs()
    message = (RH * TILE + PAD, TILE)
    a_tiles, b_tiles = a_tiles.reshape(SECTIONS * KA * TILE, TILE), b_tiles.reshape(KB * TILE, TILE)
    *quarters, left = messages(left_kernel, [message] * X, X, a_index, a_count, a_tiles)
    (right,) = messages(right_kernel, [(HALVES, *message)], HALVES, b_index, b_count, b_tiles)
    for q in (1, 0, 2):
        with jax.named_scope("left_scatter"):
            left = left + lax.ppermute(quarters[q], "col", [(col_of(Y_HI - 1, X - 1), col_of(Y_HI - 1, q))])

    def right_send(array, pairs):
        with jax.named_scope("right_step"):
            return lax.ppermute(array, "row", [(row_of(*a, c), row_of(*b, c)) for a, b in pairs for c in range(CORE)])

    def right_step(array, ops):
        return sum([right_send(array, pairs) for pairs in ops], array)

    along = [right_send(right[h], right_steps(h)[0][0]) for h in range(HALVES)]
    right = right_step(right, [[((1, Z - 1), (0, Z - 1))]])
    mine = [after(right[h] + along[h], left) for h in range(HALVES)]
    c_partial = after(c_partial, left)
    with jax.named_scope("left_y"):
        left = left + lax.ppermute(left, both, first)
    mine = [right_step(mine[h], right_steps(h)[1]) for h in range(HALVES)]
    held = hold(c_partial)
    mine = [after(half, left, held) for half in mine]
    with jax.named_scope("left_y"):
        left = left + lax.ppermute(left, both, second)
    mine = [right_step(mine[h], right_steps(h)[2]) for h in range(HALVES)]
    mine = [after(half, left) for half in mine]
    lefts = [left]
    for d in range(1, X):
        with jax.named_scope("left_x"):
            pairs = [(col_of(y, x_), col_of(y, (x_ + d) % X)) for y in range(Y_HI) for x_ in range(X)]
            lefts.append(lax.ppermute(left, "col", pairs))
    with jax.named_scope("right_core"):
        other = lax.ppermute(jnp.stack(mine), "row", [(r, r ^ 1) for r in range(N_ROW)])
    return lefts, [*mine, other], held


def hold_kernel(c_ref, held_ref):
    held_ref[...] = c_ref[...]


def hold(c_partial):
    vmem = pl.BlockSpec(memory_space=pltpu.VMEM)
    return pl.pallas_call(
        hold_kernel,
        out_shape=jax.ShapeDtypeStruct((MB * TILE, NB * TILE), jnp.float32),
        in_specs=[vmem],
        out_specs=vmem,
        compiler_params=pltpu.CompilerParams(vmem_limit_bytes=4 * 1024 * 1024),
    )(c_partial)


def product_kernel(slot_ref, table_ref, mask_ref, *refs):
    lefts, (*mine, other_ref), (held_ref, kept_ref, sum_ref) = refs[:X], refs[X : X + HALVES + 1], refs[X + HALVES + 1 :]
    rights = [*mine, *(other_ref.at[h] for h in range(HALVES))]
    kept_ref[...] = held_ref[...]
    core, x = lax.axis_index("row") % CORE, lax.axis_index("col") % X
    for d, left_ref in enumerate(lefts):
        section = ((x + X - d) % X) // (X // SECTIONS)
        which = jnp.where(section == core, 0, 1)

        def step(t, carry):
            slot = slot_ref[d * LQ + t]

            @pl.when(slot >= 0)
            def _():
                rows = pl.ds(pl.multiple_of((slot // W) * TILE, TILE), TILE)
                tile = pl.ds(pl.multiple_of(t * TILE, TILE), TILE)
                for n in range(NB):
                    p = table_ref[which * W * NB + (slot % W) * NB + n]

                    @pl.when(p >= 0)
                    def _():
                        for r in range(2 * HALVES):

                            @pl.when(which * HALVES + p // RH == r)
                            def _():
                                right = rights[r][pl.ds(pl.multiple_of((p % RH) * TILE, TILE), TILE), :]
                                columns = pl.ds(n * TILE, TILE)
                                kept_ref[rows, columns] += jnp.dot(
                                    left_ref[tile, :], right, preferred_element_type=jnp.float32
                                )

            return carry

        lax.fori_loop(0, LQ, step, 0)

    sum_ref[...] = jnp.zeros_like(sum_ref)
    for n in range(NB):
        columns = pl.ds(n * TILE, TILE)
        total = jnp.zeros((1, TILE), jnp.float32)
        for m in range(MB):
            rows = pl.ds(m * TILE, TILE)
            value = kept_ref[rows, columns]
            value = value * value * mask_ref[m * NB + n].astype(jnp.float32)
            kept_ref[rows, columns] = value
            total = total + jnp.sum(value, axis=0, keepdims=True)
        sum_ref[n : n + 1, :] = total


def product(slot, table, mask, lefts, rights, held):
    smem = pl.BlockSpec(memory_space=pltpu.SMEM)
    vmem = pl.BlockSpec(memory_space=pltpu.VMEM)
    return pl.pallas_call(
        product_kernel,
        out_shape=(
            jax.ShapeDtypeStruct((MB * TILE, NB * TILE), jnp.float32),
            jax.ShapeDtypeStruct((8, TILE), jnp.float32),
        ),
        in_specs=[smem] * 3 + [vmem] * (len(lefts) + len(rights) + 1),
        out_specs=(vmem, vmem),
        input_output_aliases={3 + len(lefts) + len(rights): 0},
        compiler_params=pltpu.CompilerParams(vmem_limit_bytes=6 * 1024 * 1024),
    )(slot, table, mask, *lefts, *rights, held)


def local(a_tiles, a_index, a_count, b_tiles, b_index, b_count, c_partial, prune_mask):
    lefts, rights, held = panels_everywhere(a_tiles, a_index, a_count, b_tiles, b_index, b_count, c_partial)
    *mine, other = rights
    facing = jnp.stack([slots_of(right[None], RH) for right in (*mine, *other)]).reshape(2, 1, KB)
    hit = facing == jnp.arange(W * NB)[None, :, None]
    table = jnp.max(jnp.where(hit, jnp.arange(KB)[None, None, :], -1), axis=2).reshape(-1)
    slot = jnp.stack([slots_of(left[None], LQ) for left in lefts]).reshape(-1)
    kept, partial = product(slot, table, prune_mask.reshape(-1), lefts, rights, held)
    total = jnp.sum(gather(partial, "row", CY_GROUPS), axis=0)
    total = jnp.sum(gather(total, "row", Z_GROUPS), axis=0)
    return kept * (ROWS / total[:NB]).reshape(1, NB * TILE)


def solution(mesh):
    return jax.shard_map(
        local,
        mesh=mesh,
        in_specs=(
            P("row", "col", None, None, None, None),
            P("row", "col", None, None),
            P("row", "col", None),
            P("row", "col", None, None, None),
            P("row", "col", None),
            P("row", "col"),
            P("row", "col"),
            P("row", "col"),
        ),
        out_specs=P("row", "col"),
        check_vma=False,
    )
```

```python
import jax
import jax.numpy as jnp
from jax import lax
from jax.experimental import pallas as pl
from jax.experimental.pallas import tpu as pltpu
from jax.sharding import PartitionSpec as P

MB = 4
NB = 4
W = 32
KA = 16
KB = 16
SECTIONS = 2
TILE = 128
ROWS = 16384
Y_LO, Z, CORE = 2, 8, 2
Y_HI, X = 4, 4
N_ROW, N_COL = Y_LO * Z * CORE, Y_HI * X
LQ = SECTIONS * KA // X
HALVES = 2
RH = KB // HALVES
PAD = 16


def row_of(y_lo, z, core):
    return (y_lo * Z + z) * CORE + core


def col_of(y_hi, x):
    return y_hi * X + x


def flat(row, col):
    return row * N_COL + col


def slots_of(got, per):
    return got[:, per * TILE, :per].astype(jnp.int32).reshape(-1)


Z_GROUPS = [[row_of(y, z, c) for z in range(Z)] for y in range(Y_LO) for c in range(CORE)]
CY_GROUPS = [[row_of(y, z, c) for y in range(Y_LO) for c in range(CORE)] for z in range(Z)]


def gather(array, axis, groups):
    n = len(groups[0])
    return lax.all_to_all(jnp.broadcast_to(array, (n,) + array.shape), axis, 0, 0, axis_index_groups=groups)


def y_pairs():
    first, second = [], []
    for z in range(Z):
        for c in range(CORE):
            for x in range(X):
                lo = lambda y: flat(row_of(0, z, c), col_of(y, x))
                hi = lambda y: flat(row_of(1, z, c), col_of(y, x))
                first += [(lo(3), lo(0)), (hi(3), hi(2))]
                second += [(lo(3), lo(2)), (lo(0), lo(1)), (hi(3), hi(0)), (hi(2), hi(1))]
    return first, second


def after(array, *others):
    return lax.optimization_barrier((array, *others))[0]


SHIFTS = (0, 1, 3, 2)


def fill(tiles_ref, message_refs, slot_of, sems):
    rows = RH * TILE
    lane = lax.broadcasted_iota(jnp.int32, (PAD, TILE), 1)
    copies = [
        pltpu.make_async_copy(tiles_ref.at[pl.ds(i * rows, rows), :], ref.at[pl.ds(0, rows), :], sems.at[i])
        for i, ref in enumerate(message_refs)
    ]
    for copy in copies:
        copy.start()
    for i, ref in enumerate(message_refs):
        line = jnp.full((PAD, TILE), -1, jnp.int32)
        for t in range(RH):
            line = jnp.where(lane == t, slot_of(i * RH + t), line)
        ref[pl.ds(rows, PAD), :] = line.astype(jnp.float32).astype(jnp.bfloat16)
    for copy in copies:
        copy.wait()


def left_kernel(index_ref, count_ref, tiles_ref, *refs):
    *quarter_refs, own_ref, sems = refs
    own = lax.axis_index("col") == N_COL - 1

    @pl.when(own)
    def _():
        def slot_of(i):
            section, place = divmod(i, KA)
            return jnp.where(place < count_ref[section], index_ref[section * KA + place], -1)

        fill(tiles_ref, (*quarter_refs, own_ref), slot_of, sems)

    @pl.when(jnp.logical_not(own))
    def _():
        own_ref[...] = jnp.zeros_like(own_ref)


def right_kernel(index_ref, count_ref, tiles_ref, right_ref, sems):
    root = lax.axis_index("row") >= N_ROW - CORE

    @pl.when(root)
    def _():
        def slot_of(i):
            return jnp.where(i < count_ref[0], index_ref[i], -1)

        fill(tiles_ref, [right_ref.at[h] for h in range(HALVES)], slot_of, sems)

    @pl.when(jnp.logical_not(root))
    def _():
        right_ref[...] = jnp.zeros_like(right_ref)


def messages(kernel, shapes, copies, index, count, tiles):
    smem = pl.BlockSpec(memory_space=pltpu.SMEM)
    return pl.pallas_call(
        kernel,
        out_shape=[jax.ShapeDtypeStruct(shape, jnp.bfloat16) for shape in shapes],
        in_specs=[smem, smem, pl.BlockSpec(memory_space=pl.ANY)],
        out_specs=[pl.BlockSpec(memory_space=pltpu.VMEM)] * len(shapes),
        scratch_shapes=[pltpu.SemaphoreType.DMA((copies,))],
        compiler_params=pltpu.CompilerParams(vmem_limit_bytes=4 * 1024 * 1024),
    )(index.reshape(-1), count.reshape(-1), tiles)


def right_steps(h):
    def pairs(*moves):
        def at(y, place):
            return y, (Z - 1 + (place if h == 0 else -place)) % Z

        return [(at(y, a), at(to, b)) for y, a, to, b in moves]

    both = [(y, a, y, b) for a, b in ((0, 1), (6, 7), (4, 5), (3, 2)) for y in range(Y_LO)]
    return [
        [pairs((1, 0, 1, 3))],
        [pairs((1, 0, 1, 6), (0, 0, 0, 6), (1, 3, 1, 4)), pairs((1, 3, 0, 3), (0, 0, 0, 4))],
        [pairs(*both)],
    ]


def panels_everywhere(a_tiles, a_index, a_count, b_tiles, b_index, b_count, c_partial):
    both = ("row", "col")
    first, second = y_pairs()
    message = (RH * TILE + PAD, TILE)
    a_tiles, b_tiles = a_tiles.reshape(SECTIONS * KA * TILE, TILE), b_tiles.reshape(KB * TILE, TILE)
    *quarters, left = messages(left_kernel, [message] * X, X, a_index, a_count, a_tiles)
    (right,) = messages(right_kernel, [(HALVES, *message)], HALVES, b_index, b_count, b_tiles)
    for q in (1, 0, 2):
        with jax.named_scope("left_scatter"):
            left = left + lax.ppermute(quarters[q], "col", [(col_of(Y_HI - 1, X - 1), col_of(Y_HI - 1, q))])

    def right_send(array, pairs):
        with jax.named_scope("right_step"):
            return lax.ppermute(array, "row", [(row_of(*a, c), row_of(*b, c)) for a, b in pairs for c in range(CORE)])

    def right_step(array, ops):
        return sum([right_send(array, pairs) for pairs in ops], array)

    along = [right_send(right[h], right_steps(h)[0][0]) for h in range(HALVES)]
    right = right_step(right, [[((1, Z - 1), (0, Z - 1))]])
    mine = [after(right[h] + along[h], left) for h in range(HALVES)]
    c_partial = after(c_partial, left)
    with jax.named_scope("left_y"):
        left = left + lax.ppermute(left, both, first)
    mine = [right_step(mine[h], right_steps(h)[1]) for h in range(HALVES)]
    held = hold(c_partial)
    mine = [after(half, left, held) for half in mine]
    with jax.named_scope("left_y"):
        left = left + lax.ppermute(left, both, second)
    mine = [right_step(mine[h], right_steps(h)[2]) for h in range(HALVES)]
    mine = [after(half, left) for half in mine]
    lefts = [left]
    for d in SHIFTS[1:]:
        with jax.named_scope("left_x"):
            pairs = [(col_of(y, x_), col_of(y, (x_ + d) % X)) for y in range(Y_HI) for x_ in range(X)]
            lefts.append(lax.ppermute(left, "col", pairs))
    with jax.named_scope("right_core"):
        other = lax.ppermute(jnp.stack(mine), "row", [(r, r ^ 1) for r in range(N_ROW)])
    return lefts, [*mine, other], held


def hold_kernel(c_ref, held_ref):
    held_ref[...] = c_ref[...]


def hold(c_partial):
    vmem = pl.BlockSpec(memory_space=pltpu.VMEM)
    return pl.pallas_call(
        hold_kernel,
        out_shape=jax.ShapeDtypeStruct((MB * TILE, NB * TILE), jnp.float32),
        in_specs=[vmem],
        out_specs=vmem,
        compiler_params=pltpu.CompilerParams(vmem_limit_bytes=4 * 1024 * 1024),
    )(c_partial)


def product_kernel(slot_ref, table_ref, mask_ref, *refs):
    lefts, (*mine, other_ref), (held_ref, kept_ref, sum_ref) = refs[:X], refs[X : X + HALVES + 1], refs[X + HALVES + 1 :]
    rights = [*mine, *(other_ref.at[h] for h in range(HALVES))]
    kept_ref[...] = held_ref[...]
    core, x = lax.axis_index("row") % CORE, lax.axis_index("col") % X
    for i, (d, left_ref) in enumerate(zip(SHIFTS, lefts)):
        section = ((x + X - d) % X) // (X // SECTIONS)
        which = jnp.where(section == core, 0, 1)

        def step(t, carry):
            slot = slot_ref[i * LQ + t]

            @pl.when(slot >= 0)
            def _():
                rows = pl.ds(pl.multiple_of((slot // W) * TILE, TILE), TILE)
                tile = pl.ds(pl.multiple_of(t * TILE, TILE), TILE)
                for n in range(NB):
                    p = table_ref[which * W * NB + (slot % W) * NB + n]

                    @pl.when(p >= 0)
                    def _():
                        for r in range(2 * HALVES):

                            @pl.when(which * HALVES + p // RH == r)
                            def _():
                                right = rights[r][pl.ds(pl.multiple_of((p % RH) * TILE, TILE), TILE), :]
                                columns = pl.ds(n * TILE, TILE)
                                kept_ref[rows, columns] += jnp.dot(
                                    left_ref[tile, :], right, preferred_element_type=jnp.float32
                                )

            return carry

        lax.fori_loop(0, LQ, step, 0)

    sum_ref[...] = jnp.zeros_like(sum_ref)
    for n in range(NB):
        columns = pl.ds(n * TILE, TILE)
        total = jnp.zeros((1, TILE), jnp.float32)
        for m in range(MB):
            rows = pl.ds(m * TILE, TILE)
            value = kept_ref[rows, columns]
            value = value * value * mask_ref[m * NB + n].astype(jnp.float32)
            kept_ref[rows, columns] = value
            total = total + jnp.sum(value, axis=0, keepdims=True)
        sum_ref[n : n + 1, :] = total


def product(slot, table, mask, lefts, rights, held):
    smem = pl.BlockSpec(memory_space=pltpu.SMEM)
    vmem = pl.BlockSpec(memory_space=pltpu.VMEM)
    return pl.pallas_call(
        product_kernel,
        out_shape=(
            jax.ShapeDtypeStruct((MB * TILE, NB * TILE), jnp.float32),
            jax.ShapeDtypeStruct((8, TILE), jnp.float32),
        ),
        in_specs=[smem] * 3 + [vmem] * (len(lefts) + len(rights) + 1),
        out_specs=(vmem, vmem),
        input_output_aliases={3 + len(lefts) + len(rights): 0},
        compiler_params=pltpu.CompilerParams(vmem_limit_bytes=6 * 1024 * 1024),
    )(slot, table, mask, *lefts, *rights, held)


def local(a_tiles, a_index, a_count, b_tiles, b_index, b_count, c_partial, prune_mask):
    lefts, rights, held = panels_everywhere(a_tiles, a_index, a_count, b_tiles, b_index, b_count, c_partial)
    *mine, other = rights
    facing = jnp.stack([slots_of(right[None], RH) for right in (*mine, *other)]).reshape(2, 1, KB)
    hit = facing == jnp.arange(W * NB)[None, :, None]
    table = jnp.max(jnp.where(hit, jnp.arange(KB)[None, None, :], -1), axis=2).reshape(-1)
    slot = jnp.stack([slots_of(left[None], LQ) for left in lefts]).reshape(-1)
    kept, partial = product(slot, table, prune_mask.reshape(-1), lefts, rights, held)
    total = jnp.sum(gather(partial, "row", CY_GROUPS), axis=0)
    total = jnp.sum(gather(total, "row", Z_GROUPS), axis=0)
    return kept * (ROWS / total[:NB]).reshape(1, NB * TILE)


def solution(mesh):
    return jax.shard_map(
        local,
        mesh=mesh,
        in_specs=(
            P("row", "col", None, None, None, None),
            P("row", "col", None, None),
            P("row", "col", None),
            P("row", "col", None, None, None),
            P("row", "col", None),
            P("row", "col"),
            P("row", "col"),
            P("row", "col"),
        ),
        out_specs=P("row", "col"),
        check_vma=False,
    )
```

```python
import jax
import jax.numpy as jnp
from jax import lax
from jax.experimental import pallas as pl
from jax.experimental.pallas import tpu as pltpu
from jax.sharding import PartitionSpec as P

MB = 4
NB = 4
W = 32
KA = 16
KB = 16
SECTIONS = 2
TILE = 128
ROWS = 16384
Y_LO, Z, CORE = 2, 8, 2
Y_HI, X = 4, 4
N_ROW, N_COL = Y_LO * Z * CORE, Y_HI * X
LQ = SECTIONS * KA // X
HALVES = 2
RH = KB // HALVES
PAD = 16


def row_of(y_lo, z, core):
    return (y_lo * Z + z) * CORE + core


def col_of(y_hi, x):
    return y_hi * X + x


def flat(row, col):
    return row * N_COL + col


def slots_of(got, per):
    return got[:, per * TILE, :per].astype(jnp.int32).reshape(-1)


Z_GROUPS = [[row_of(y, z, c) for z in range(Z)] for y in range(Y_LO) for c in range(CORE)]
CY_GROUPS = [[row_of(y, z, c) for y in range(Y_LO) for c in range(CORE)] for z in range(Z)]


def gather(array, axis, groups):
    n = len(groups[0])
    return lax.all_to_all(jnp.broadcast_to(array, (n,) + array.shape), axis, 0, 0, axis_index_groups=groups)


def y_pairs():
    first, second = [], []
    for z in range(Z):
        for c in range(CORE):
            for x in range(X):
                lo = lambda y: flat(row_of(0, z, c), col_of(y, x))
                hi = lambda y: flat(row_of(1, z, c), col_of(y, x))
                first += [(lo(3), lo(0)), (hi(3), hi(2))]
                second += [(lo(3), lo(2)), (lo(0), lo(1)), (hi(3), hi(0)), (hi(2), hi(1))]
    return first, second


def after(array, *others):
    return lax.optimization_barrier((array, *others))[0]


SHIFTS = (0, 1, 3, 2)


def fill(tiles_ref, message_refs, slot_of, sems):
    rows = RH * TILE
    lane = lax.broadcasted_iota(jnp.int32, (PAD, TILE), 1)
    copies = [
        pltpu.make_async_copy(tiles_ref.at[pl.ds(i * rows, rows), :], ref.at[pl.ds(0, rows), :], sems.at[i])
        for i, ref in enumerate(message_refs)
    ]
    for copy in copies:
        copy.start()
    for i, ref in enumerate(message_refs):
        line = jnp.full((PAD, TILE), -1, jnp.int32)
        for t in range(RH):
            line = jnp.where(lane == t, slot_of(i * RH + t), line)
        ref[pl.ds(rows, PAD), :] = line.astype(jnp.float32).astype(jnp.bfloat16)
    for copy in copies:
        copy.wait()


def left_kernel(index_ref, count_ref, tiles_ref, *refs):
    *quarter_refs, own_ref, sems = refs
    own = lax.axis_index("col") == N_COL - 1

    @pl.when(own)
    def _():
        def slot_of(i):
            section, place = divmod(i, KA)
            return jnp.where(place < count_ref[section], index_ref[section * KA + place], -1)

        fill(tiles_ref, (*quarter_refs, own_ref), slot_of, sems)

    @pl.when(jnp.logical_not(own))
    def _():
        own_ref[...] = jnp.zeros_like(own_ref)


def right_kernel(index_ref, count_ref, tiles_ref, right_ref, sems):
    root = lax.axis_index("row") >= N_ROW - CORE

    @pl.when(root)
    def _():
        def slot_of(i):
            return jnp.where(i < count_ref[0], index_ref[i], -1)

        fill(tiles_ref, [right_ref.at[h] for h in range(HALVES)], slot_of, sems)

    @pl.when(jnp.logical_not(root))
    def _():
        right_ref[...] = jnp.zeros_like(right_ref)


def messages(kernel, shapes, copies, index, count, tiles):
    smem = pl.BlockSpec(memory_space=pltpu.SMEM)
    return pl.pallas_call(
        kernel,
        out_shape=[jax.ShapeDtypeStruct(shape, jnp.bfloat16) for shape in shapes],
        in_specs=[smem, smem, pl.BlockSpec(memory_space=pl.ANY)],
        out_specs=[pl.BlockSpec(memory_space=pltpu.VMEM)] * len(shapes),
        scratch_shapes=[pltpu.SemaphoreType.DMA((copies,))],
        compiler_params=pltpu.CompilerParams(vmem_limit_bytes=4 * 1024 * 1024),
    )(index.reshape(-1), count.reshape(-1), tiles)


def right_steps(h):
    def pairs(*moves):
        def at(y, place):
            return y, (Z - 1 + (place if h == 0 else -place)) % Z

        return [(at(y, a), at(to, b)) for y, a, to, b in moves]

    both = [(y, a, y, b) for a, b in ((0, 1), (6, 7), (4, 5), (3, 2)) for y in range(Y_LO)]
    return [
        [pairs((1, 0, 1, 3))],
        [pairs((1, 0, 1, 6), (0, 0, 0, 6), (1, 3, 1, 4)), pairs((1, 3, 0, 3), (0, 0, 0, 4))],
        [pairs(*both)],
    ]


def panels_everywhere(a_tiles, a_index, a_count, b_tiles, b_index, b_count, c_partial):
    both = ("row", "col")
    first, second = y_pairs()
    message = (RH * TILE + PAD, TILE)
    a_tiles, b_tiles = a_tiles.reshape(SECTIONS * KA * TILE, TILE), b_tiles.reshape(KB * TILE, TILE)
    a_index, a_count, b_index, b_count = lax.optimization_barrier(
        (a_index.reshape(-1), a_count.reshape(-1), b_index.reshape(-1), b_count.reshape(-1))
    )
    *quarters, left = messages(left_kernel, [message] * X, X, a_index, a_count, a_tiles)
    (right,) = messages(right_kernel, [(HALVES, *message)], HALVES, b_index, b_count, b_tiles)
    for q in (1, 0, 2):
        with jax.named_scope("left_scatter"):
            left = left + lax.ppermute(quarters[q], "col", [(col_of(Y_HI - 1, X - 1), col_of(Y_HI - 1, q))])

    def right_send(array, pairs):
        with jax.named_scope("right_step"):
            return lax.ppermute(array, "row", [(row_of(*a, c), row_of(*b, c)) for a, b in pairs for c in range(CORE)])

    def right_step(array, ops):
        return sum([right_send(array, pairs) for pairs in ops], array)

    along = [right_send(right[h], right_steps(h)[0][0]) for h in range(HALVES)]
    right = right_step(right, [[((1, Z - 1), (0, Z - 1))]])
    mine = [after(right[h] + along[h], left) for h in range(HALVES)]
    c_partial = after(c_partial, left)
    with jax.named_scope("left_y"):
        left = left + lax.ppermute(left, both, first)
    mine = [right_step(mine[h], right_steps(h)[1]) for h in range(HALVES)]
    held = hold(c_partial)
    mine = [after(half, left, held) for half in mine]
    with jax.named_scope("left_y"):
        left = left + lax.ppermute(left, both, second)
    mine = [right_step(mine[h], right_steps(h)[2]) for h in range(HALVES)]
    mine = [after(half, left) for half in mine]
    lefts = [left]
    for d in SHIFTS[1:]:
        with jax.named_scope("left_x"):
            pairs = [(col_of(y, x_), col_of(y, (x_ + d) % X)) for y in range(Y_HI) for x_ in range(X)]
            lefts.append(lax.ppermute(left, "col", pairs))
    with jax.named_scope("right_core"):
        other = lax.ppermute(jnp.stack(mine), "row", [(r, r ^ 1) for r in range(N_ROW)])
    return lefts, [*mine, other], held


def hold_kernel(c_ref, held_ref):
    held_ref[...] = c_ref[...]


def hold(c_partial):
    vmem = pl.BlockSpec(memory_space=pltpu.VMEM)
    return pl.pallas_call(
        hold_kernel,
        out_shape=jax.ShapeDtypeStruct((MB * TILE, NB * TILE), jnp.float32),
        in_specs=[vmem],
        out_specs=vmem,
        compiler_params=pltpu.CompilerParams(vmem_limit_bytes=4 * 1024 * 1024),
    )(c_partial)


def product_kernel(slot_ref, table_ref, mask_ref, *refs):
    lefts, (*mine, other_ref), (held_ref, kept_ref, sum_ref) = refs[:X], refs[X : X + HALVES + 1], refs[X + HALVES + 1 :]
    rights = [*mine, *(other_ref.at[h] for h in range(HALVES))]
    kept_ref[...] = held_ref[...]
    core, x = lax.axis_index("row") % CORE, lax.axis_index("col") % X
    for i, (d, left_ref) in enumerate(zip(SHIFTS, lefts)):
        section = ((x + X - d) % X) // (X // SECTIONS)
        which = jnp.where(section == core, 0, 1)

        def step(t, carry):
            slot = slot_ref[i * LQ + t]

            @pl.when(slot >= 0)
            def _():
                rows = pl.ds(pl.multiple_of((slot // W) * TILE, TILE), TILE)
                tile = pl.ds(pl.multiple_of(t * TILE, TILE), TILE)
                for n in range(NB):
                    p = table_ref[which * W * NB + (slot % W) * NB + n]

                    @pl.when(p >= 0)
                    def _():
                        for r in range(2 * HALVES):

                            @pl.when(which * HALVES + p // RH == r)
                            def _():
                                right = rights[r][pl.ds(pl.multiple_of((p % RH) * TILE, TILE), TILE), :]
                                columns = pl.ds(n * TILE, TILE)
                                kept_ref[rows, columns] += jnp.dot(
                                    left_ref[tile, :], right, preferred_element_type=jnp.float32
                                )

            return carry

        lax.fori_loop(0, LQ, step, 0)

    sum_ref[...] = jnp.zeros_like(sum_ref)
    for n in range(NB):
        columns = pl.ds(n * TILE, TILE)
        total = jnp.zeros((1, TILE), jnp.float32)
        for m in range(MB):
            rows = pl.ds(m * TILE, TILE)
            value = kept_ref[rows, columns]
            value = value * value * mask_ref[m * NB + n].astype(jnp.float32)
            kept_ref[rows, columns] = value
            total = total + jnp.sum(value, axis=0, keepdims=True)
        sum_ref[n : n + 1, :] = total


def product(slot, table, mask, lefts, rights, held):
    smem = pl.BlockSpec(memory_space=pltpu.SMEM)
    vmem = pl.BlockSpec(memory_space=pltpu.VMEM)
    return pl.pallas_call(
        product_kernel,
        out_shape=(
            jax.ShapeDtypeStruct((MB * TILE, NB * TILE), jnp.float32),
            jax.ShapeDtypeStruct((8, TILE), jnp.float32),
        ),
        in_specs=[smem] * 3 + [vmem] * (len(lefts) + len(rights) + 1),
        out_specs=(vmem, vmem),
        input_output_aliases={3 + len(lefts) + len(rights): 0},
        compiler_params=pltpu.CompilerParams(vmem_limit_bytes=6 * 1024 * 1024),
    )(slot, table, mask, *lefts, *rights, held)


def local(a_tiles, a_index, a_count, b_tiles, b_index, b_count, c_partial, prune_mask):
    lefts, rights, held = panels_everywhere(a_tiles, a_index, a_count, b_tiles, b_index, b_count, c_partial)
    *mine, other = rights
    facing = jnp.stack([slots_of(right[None], RH) for right in (*mine, *other)]).reshape(2, 1, KB)
    hit = facing == jnp.arange(W * NB)[None, :, None]
    table = jnp.max(jnp.where(hit, jnp.arange(KB)[None, None, :], -1), axis=2).reshape(-1)
    slot = jnp.stack([slots_of(left[None], LQ) for left in lefts]).reshape(-1)
    kept, partial = product(slot, table, prune_mask.reshape(-1), lefts, rights, held)
    total = jnp.sum(gather(partial, "row", CY_GROUPS), axis=0)
    total = jnp.sum(gather(total, "row", Z_GROUPS), axis=0)
    return kept * (ROWS / total[:NB]).reshape(1, NB * TILE)


def solution(mesh):
    return jax.shard_map(
        local,
        mesh=mesh,
        in_specs=(
            P("row", "col", None, None, None, None),
            P("row", "col", None, None),
            P("row", "col", None),
            P("row", "col", None, None, None),
            P("row", "col", None),
            P("row", "col"),
            P("row", "col"),
            P("row", "col"),
        ),
        out_specs=P("row", "col"),
        check_vma=False,
    )
```
